32 devices in a mesh: vocab: 8 (over z, x), req: 4 (over y, core).
Axes of the slice: x: 2, y: 2, z: 4, core: 2. Of those that a mesh axis runs over, the one named last changes fastest.
Arguments:
- hidden: bfloat16 [1024, 2048], P(('vocab', 'req')), may hold values from -60 to 60
- positions: int32 [256], P(('vocab', 'req')), may hold values from 0 to 31
- token_ids: int32 [256], P(('vocab', 'req')), may hold values from 0 to 163839
- lengths: int32 [32], P(('vocab', 'req')), may hold values from 1 to 8
- norm_gain: float32 [2048], replicated, may hold values from 0.5 to 1.5
- head_weight: bfloat16 [2048, 163840], P('req', 'vocab'), may hold values from -0.5 to 0.5
Outputs:
- logprob: float32 [256], P(('vocab', 'req'))
- entropy: float32 [256], P(('vocab', 'req'))
- hidden_norm: float32 [256], P(('vocab', 'req'))
- top_logit: float32 [256], P(('vocab', 'req'))
The draws below stay inside these ranges and needn't reach their ends.
All inputs are finite; a program needn't handle non-finite values.
Results may differ from the reference program's by a relative error of at most 0.00086.
Values may be sent and summed in bfloat16 or wider, within the bound.
A program may use at most 192 MiB of HBM per device.

```python
import math
import jax
import jax.numpy as jnp
import numpy as np
from jax import lax

D = 2048
V = 163840
SLOTS = 8
OWN_ROWS = 32
OWNERS = 32
HROWS = 1024
SCORED = 256


def draw_hidden(key, part):
    first, second = jax.random.split(jax.random.fold_in(key, 1), 2)
    scales = jnp.exp(jax.random.uniform(second, (HROWS, 1), jnp.float32) * jnp.log(10.0))
    base = jnp.clip(jax.random.normal(first, (HROWS, D), jnp.float32), -6.0, 6.0)
    return jnp.clip(base * scales, -60.0, 60.0).astype(jnp.bfloat16)


def draw_head_weight(key, part):
    first = jax.random.fold_in(jax.random.fold_in(key, 2), 0)
    scale = 3.0 / jnp.sqrt(jnp.float32(D))
    weight = jnp.clip(jax.random.normal(first, (D, V), jnp.float32) * scale, -0.45, 0.45)
    return weight.astype(jnp.bfloat16)


def draw_lengths(key, part):
    drawn = jax.random.randint(jax.random.fold_in(key, 3), (OWNERS,), 1, SLOTS + 1)
    return drawn.at[0].set(SLOTS).astype(jnp.int32)


def place_ends(array, rng, low, high):
    dims = array.shape
    index_at = [jax.random.randint(jax.random.fold_in(rng, axis), (), 0, dims[axis]) for axis in range(len(dims))]
    array = array.at[tuple(index_at)].set(low)
    longest = dims.index(max(dims))
    index_at[longest] = (index_at[longest] + 1) % dims[longest]
    return array.at[tuple(index_at)].set(high)


def skewed_wide(own_key, dims, count, slope):
    loads = [min(1 << octave, count + 1 - (1 << octave)) * (1 << 20) // math.isqrt((1 << octave) ** slope) + 1 for octave in range((count + 1).bit_length()) if 1 << octave <= count]
    deviation = 1 + sum(loads) // (1 << 30)
    listing = np.cumsum(np.array([max(1, weight // deviation) for weight in loads]))
    lot = jax.random.randint(jax.random.fold_in(own_key, 1), dims, 0, int(listing[len(loads) - 1]))
    start = jnp.left_shift(1, jnp.searchsorted(jnp.asarray(listing, jnp.int32), lot, side="right").astype(jnp.int32))
    rank = start - 1 + jax.random.randint(jax.random.fold_in(own_key, 4), dims, 0, 1 << 30) % jnp.minimum(start, count + 1 - start)
    return jax.random.permutation(jax.random.fold_in(own_key, 2), count)[rank].astype(jnp.int32)


def setup_inputs(seed: int = 0) -> dict:
    seeds = jax.random.split(jax.random.key(seed), 7)
    return {
        "hidden": draw_hidden(jax.random.fold_in(seeds[6], 71), 0),
        "positions": place_ends(jax.random.randint(seeds[1], (SCORED,), 0, OWN_ROWS), jax.random.fold_in(seeds[1], 1), 0, OWN_ROWS - 1).astype(jnp.int32),
        "token_ids": place_ends(skewed_wide(seeds[2], (SCORED,), V, 2), jax.random.fold_in(seeds[2], 3), 0, V - 1).astype(jnp.int32),
        "lengths": draw_lengths(jax.random.fold_in(seeds[6], 71), 0),
        "norm_gain": jnp.clip(1.0 + 0.1 * jax.random.normal(seeds[4], (D,), jnp.float32), 0.5, 1.5),
        "head_weight": draw_head_weight(jax.random.fold_in(seeds[6], 71), 0),
    }


def block_stats(rows, ids, head_weight):
    logits = jnp.dot(rows, head_weight, preferred_element_type=jnp.float32)
    top = lax.optimization_barrier(jnp.max(logits, axis=1))
    expo = jnp.exp(logits - top[:, None])
    total = lax.optimization_barrier(jnp.sum(expo, axis=1))
    weighted = lax.optimization_barrier(jnp.sum(expo * logits, axis=1))
    chosen = jnp.take_along_axis(logits, ids[:, None].astype(jnp.int32), axis=1)[:, 0]
    return (top, total, weighted, chosen)

def reference(hidden, positions, token_ids, lengths, norm_gain, head_weight):
    owners = lengths.shape[0]
    slots = positions.shape[0] // owners
    width = hidden.shape[1]
    grouped = hidden.reshape(owners, hidden.shape[0] // owners, width)
    where = positions.reshape(owners, slots).astype(jnp.int32)
    picked = jnp.take_along_axis(grouped, where[:, :, None], axis=1).reshape(-1, width).astype(jnp.float32)
    square_mean = lax.optimization_barrier(jnp.mean(picked * picked, axis=1))
    normed = (picked * lax.rsqrt(square_mean + 1e-05)[:, None] * norm_gain[None, :]).astype(jnp.bfloat16)
    count = normed.shape[0]
    blk = 32
    rows_b = normed.reshape(count // blk, blk, width)
    ids_b = token_ids.reshape(count // blk, blk)
    top, total, weighted, chosen = lax.map(lambda a: block_stats(a[0], a[1], head_weight), (rows_b, ids_b))
    top = top.reshape(-1)
    total = total.reshape(-1)
    weighted = weighted.reshape(-1)
    chosen = chosen.reshape(-1)
    lse = top + jnp.log(total)
    slot_index = jnp.arange(count, dtype=jnp.int32) % slots
    owner_len = jnp.repeat(lengths.astype(jnp.int32), slots)
    live = (slot_index < owner_len).astype(jnp.float32)
    logprob = live * (chosen - lse)
    entropy = live * (lse - weighted / total)
    hidden_norm = live * jnp.sqrt(square_mean)
    top_logit = live * top
    return (logprob, entropy, hidden_norm, top_logit)
```

```python
import functools

import jax
import jax.numpy as jnp
from jax import lax
from jax.experimental import pallas as pl
from jax.experimental.pallas import tpu as pltpu
from jax.sharding import PartitionSpec as P

MESH = pl.DeviceIdType.MESH
F32 = jnp.float32
BF16 = jnp.bfloat16
LANES = 128
TILE = 512
RING = 6
STEPS = 32000.0
CAPS = (128, 144, 160, 176, 192)
VMEM_LIMIT = 58 * 1024 * 1024


def everyone(total, groups, me, act):
    def step(i, carry):
        target = lax.rem(me + i, total)
        act(i, target, (target // groups, lax.rem(target, groups)))
        return carry

    lax.fori_loop(1, total, step, 0)


def greet(total, groups, me):
    barrier = pltpu.get_barrier_semaphore()
    everyone(
        total,
        groups,
        me,
        lambda i, target, place: pl.semaphore_signal(
            barrier, inc=1, device_id=place, device_id_type=MESH
        ),
    )
    return barrier


def gather_kernel(
    total, groups, caps,
    hidden, positions, ids, lengths, gain,
    rows_out, meta_out, rank_out, own_out, bucket_out,
    message, inbox, send_sem, recv_sem,
):
    v, r = lax.axis_index("vocab"), lax.axis_index("req")
    me = v * groups + r
    barrier = greet(total, groups, me)

    slots = positions.shape[0]
    width = hidden.shape[1]
    part = width // groups
    half = part // 2
    hot = lax.broadcasted_iota(jnp.int32, (slots, hidden.shape[0]), 1) == positions[...]
    picked = jnp.dot(
        hot.astype(F32), hidden[...].astype(F32), preferred_element_type=F32
    )
    square_mean = jnp.sum(picked * picked, axis=1, keepdims=True) * (1.0 / width)
    normed = picked * lax.rsqrt(square_mean + 1e-05) * gain[...]
    normed = normed.astype(BF16).astype(F32)
    grain = []
    for side in range(2):
        bound = jnp.sum(
            jnp.abs(normed[:, side * (width // 2) : (side + 1) * (width // 2)]),
            axis=1, keepdims=True,
        )
        grain.append(bound * (0.5 * (1.0 + 2.0**-7) / STEPS) + 1e-30)
    lane = lax.broadcasted_iota(jnp.int32, (slots, LANES), 1)
    token = ids[...]
    length = lengths[...]
    meta = jnp.zeros((slots, LANES), F32)
    for place, value in enumerate(
        (
            (token & 255).astype(F32),
            ((token >> 8) & 255).astype(F32),
            (token >> 16).astype(F32),
            length.astype(F32),
            grain[0],
            grain[1],
        )
    ):
        meta = jnp.where(lane == place, value, meta)
    meta = jnp.concatenate([meta, jnp.zeros((slots, LANES), F32)], axis=0).astype(BF16)
    for g in range(groups):
        message[g, :, :half] = jnp.concatenate(
            [
                normed[:, g * part : g * part + half],
                normed[:, g * part + half : (g + 1) * part],
            ],
            axis=0,
        ).astype(BF16)
        message[g, :, half:] = meta
    slot = lax.broadcasted_iota(jnp.int32, (slots, LANES), 0)
    alive = (slot < length).astype(F32)
    own_out[...] = jnp.where(lane == 0, square_mean, alive)

    pl.semaphore_wait(barrier, total - 1)

    def copy_to(i, target, place):
        return pltpu.make_async_remote_copy(
            src_ref=message.at[place[1]],
            dst_ref=inbox.at[me],
            send_sem=send_sem.at[i],
            recv_sem=recv_sem.at[me],
            device_id=place,
            device_id_type=MESH,
        )

    def copy_from(i, target, place):
        return pltpu.make_async_remote_copy(
            src_ref=message.at[place[1]],
            dst_ref=inbox.at[target],
            send_sem=send_sem.at[i],
            recv_sem=recv_sem.at[target],
            device_id=place,
            device_id_type=MESH,
        )

    everyone(total, groups, me, lambda *a: copy_to(*a).start())
    inbox[me] = message[r]
    everyone(total, groups, me, lambda *a: copy_from(*a).wait_recv())

    count = total * slots
    got = inbox[...].astype(F32)
    rows = jnp.concatenate(
        [
            got[:, :slots, :half].reshape(count, half),
            got[:, slots:, :half].reshape(count, half),
        ],
        axis=1,
    ).astype(BF16)
    info = got[:, :slots, half:].reshape(count, LANES)
    at = lax.rem(lax.broadcasted_iota(jnp.int32, (count, LANES), 0), slots).astype(F32)
    live = (at < info[:, 3:4]).astype(F32)
    across = lax.broadcasted_iota(jnp.int32, (count, count), 0)
    along = lax.broadcasted_iota(jnp.int32, (count, count), 1)
    live_row = live.T
    rank_row = jnp.dot(
        live_row.astype(BF16), (across < along).astype(F32).astype(BF16),
        preferred_element_type=F32,
    )
    rank_col = jnp.dot(
        (along < across).astype(F32).astype(BF16), live.astype(BF16),
        preferred_element_type=F32,
    )
    rank_out[...] = jnp.where(live > 0.0, rank_col, -1.0)
    goes = jnp.where(live_row[0:1, :] > 0.0, rank_row[0:1, :], -1.0)
    order = (goes == across.astype(F32)).astype(F32).astype(BF16)
    rows_out[...] = jnp.dot(order, rows, preferred_element_type=F32).astype(BF16)
    meta_out[...] = jnp.dot(order, info.astype(BF16), preferred_element_type=F32)
    lives = jnp.sum(live_row[0:1, :]).astype(jnp.int32)
    bucket = jnp.int32(0)
    for cap in caps[:-1]:
        bucket = bucket + (lives > cap).astype(jnp.int32)
    bucket_out[0] = bucket

    everyone(total, groups, me, lambda *a: copy_to(*a).wait_send())


def score_kernel(
    total, groups, rows, count,
    x, meta, rank, own, weight,
    out,
    ring, core_out, core_in, part, side_out, side_in, mine,
    ask, give_scale, take_scale, top, total_sum, weighted, chosen, stats, posts, mail,
    ring_sem, core_send, core_recv, side_send, side_recv, post_send, post_recv,
):
    v, r = lax.axis_index("vocab"), lax.axis_index("req")
    me = v * groups + r
    y, core = r // 2, lax.rem(r, 2)
    twin = y * 2 + (1 - core)
    across = (1 - y) * 2 + core
    diagonal = (1 - y) * 2 + (1 - core)
    columns = weight.shape[1]
    quarter = columns // groups
    tiles = quarter // TILE
    fetches = groups * tiles
    first_half = 2 * tiles

    def fetch(n):
        t = lax.rem(n, first_half) // 2
        odd = lax.rem(n, 2)
        early = (n < first_half).astype(jnp.int32)
        yy = early * (1 - y) + (1 - early) * y
        cc = odd * core + (1 - odd) * (1 - core)
        begin = pl.multiple_of((yy * 2 + cc) * quarter + t * TILE, TILE)
        where = lax.rem(n, RING)
        return pltpu.make_async_copy(
            weight.at[:, pl.ds(begin, TILE)], ring.at[where], ring_sem.at[where]
        )

    for n in range(RING - 1):
        fetch(jnp.int32(n)).start()
    barrier = greet(total, groups, me)

    lane = lax.broadcasted_iota(jnp.int32, (rows, LANES), 1)
    info = meta[:rows, :]
    token = info[:, 0:1] + info[:, 1:2] * 256.0 + info[:, 2:3] * 65536.0
    base = v * columns + r * quarter
    ask[...] = token.astype(jnp.int32) - base - lane
    low = jnp.broadcast_to(info[:, 4:5], (rows, LANES))
    high = jnp.broadcast_to(info[:, 5:6], (rows, LANES))
    is_low = jnp.broadcast_to(y == 0, (rows, LANES))
    give_scale[...] = 1.0 / jnp.where(is_low, low, high)
    take_scale[...] = jnp.where(is_low, high, low)
    top[...] = jnp.full((rows, LANES), -3e38, F32)
    total_sum[...] = jnp.zeros((rows, LANES), F32)
    weighted[...] = jnp.zeros((rows, LANES), F32)
    chosen[...] = jnp.zeros((rows, LANES), F32)
    pl.semaphore_wait(barrier, total - 1)

    def product(n):
        @pl.when(n + (RING - 1) < fetches)
        def _():
            fetch(n + (RING - 1)).start()

        fetch(n).wait()
        return jnp.dot(x[:rows, :], ring[lax.rem(n, RING)], preferred_element_type=F32)

    def core_copy(k):
        return pltpu.make_async_remote_copy(
            src_ref=core_out.at[k],
            dst_ref=core_in.at[k],
            send_sem=core_send.at[k],
            recv_sem=core_recv.at[k],
            device_id=(v, twin),
            device_id_type=MESH,
        )

    def side_copy(t):
        return pltpu.make_async_remote_copy(
            src_ref=side_out.at[t],
            dst_ref=side_in.at[t],
            send_sem=side_send.at[t],
            recv_sem=side_recv.at[t],
            device_id=(v, across),
            device_id_type=MESH,
        )

    blocks = rows // 16

    def hand_over(t):
        core_copy(t).wait_recv()
        held = lax.rem(t, 2)

        def block(b, carry):
            at = pl.ds(pl.multiple_of(b * 16, 16), 16)
            scale = give_scale[at, :]
            for c in range(TILE // LANES):
                cols = pl.ds(c * LANES, LANES)
                value = (part[held, at, cols] + core_in[t, at, cols]) * scale
                side_out[t, at, cols] = jnp.round(value).astype(jnp.int32).astype(jnp.int16)
            return carry

        lax.fori_loop(0, blocks, block, 0)
        side_copy(t).start()

    def early(t, carry):
        core_out[t] = product(2 * t)
        core_copy(t).start()
        part[lax.rem(t, 2)] = product(2 * t + 1)

        @pl.when(t > 0)
        def _():
            hand_over(t - 1)

        return carry

    lax.fori_loop(0, tiles, early, 0)
    hand_over(jnp.int32(tiles - 1))

    def late(t, carry):
        core_out[tiles + t] = product(first_half + 2 * t)
        core_copy(tiles + t).start()
        mine[t] = product(first_half + 2 * t + 1)
        return carry

    lax.fori_loop(0, tiles, late, 0)

    def tally(t, carry):
        core_copy(tiles + t).wait_recv()
        side_copy(t).wait_recv()

        def block(b, inner):
            at = pl.ds(pl.multiple_of(b * 16, 16), 16)
            scale = take_scale[at, :]
            sought = ask[at, :] - t * TILE
            values = []
            for c in range(TILE // LANES):
                cols = pl.ds(c * LANES, LANES)
                far = side_in[t, at, cols].astype(jnp.int32).astype(F32) * scale
                values.append(mine[t, at, cols] + core_in[tiles + t, at, cols] + far)
            before = top[at, :]
            peak = before
            for value in values:
                peak = jnp.maximum(peak, value)
            fade = jnp.exp(before - peak)
            one = total_sum[at, :] * fade
            two = weighted[at, :] * fade
            hit = chosen[at, :]
            for c, value in enumerate(values):
                power = jnp.exp(value - peak)
                one = one + power
                two = two + power * value
                hit = jnp.where(sought == c * LANES, value, hit)
            top[at, :] = peak
            total_sum[at, :] = one
            weighted[at, :] = two
            chosen[at, :] = hit
            return inner

        lax.fori_loop(0, blocks, block, 0)
        return carry

    lax.fori_loop(0, tiles, tally, 0)

    peak = jnp.max(top[...], axis=1, keepdims=True)
    fade = jnp.exp(top[...] - peak)
    one = jnp.sum(total_sum[...] * fade, axis=1, keepdims=True)
    two = jnp.sum(weighted[...] * fade, axis=1, keepdims=True)
    hit = jnp.sum(chosen[...], axis=1, keepdims=True)
    packed = jnp.where(lane == 0, peak, jnp.where(lane == 1, one, jnp.where(lane == 2, two, hit)))
    stats[:rows, :] = packed
    if rows < count:
        stats[rows:, :] = jnp.zeros((count - rows, LANES), F32)
    sought = lax.broadcasted_iota(jnp.int32, (count, count), 1).astype(F32)
    back = (rank[:, 0:1] == sought).astype(F32)
    spread = jnp.dot(
        back, stats[...], preferred_element_type=F32, precision=lax.Precision.HIGHEST
    )
    posts[...] = spread.reshape(posts.shape)

    def post_to(i, target, place):
        return pltpu.make_async_remote_copy(
            src_ref=posts.at[target],
            dst_ref=mail.at[me],
            send_sem=post_send.at[i],
            recv_sem=post_recv.at[me],
            device_id=place,
            device_id_type=MESH,
        )

    def post_from(i, target, place):
        return pltpu.make_async_remote_copy(
            src_ref=posts.at[target],
            dst_ref=mail.at[target],
            send_sem=post_send.at[i],
            recv_sem=post_recv.at[target],
            device_id=place,
            device_id_type=MESH,
        )

    everyone(total, groups, me, lambda *a: post_to(*a).start())
    mail[me] = posts[me]

    def sent(k, carry):
        core_copy(k).wait_send()
        return carry

    lax.fori_loop(0, 2 * tiles, sent, 0)

    def sent_side(t, carry):
        side_copy(t).wait_send()
        return carry

    lax.fori_loop(0, tiles, sent_side, 0)
    everyone(total, groups, me, lambda *a: post_from(*a).wait_recv())

    letters = mail[...]
    tops = letters[:, :, 0:1]
    peak = jnp.max(tops, axis=0)
    fade = jnp.exp(tops - peak[None])
    one = jnp.sum(letters[:, :, 1:2] * fade, axis=0)
    two = jnp.sum(letters[:, :, 2:3] * fade, axis=0)
    hit = jnp.sum(letters[:, :, 3:4], axis=0)
    lse = peak + jnp.log(one)
    alive = own[:, 1:2] > 0.0
    place = lax.broadcasted_iota(jnp.int32, out.shape, 1)
    result = jnp.where(
        place == 0,
        hit - lse,
        jnp.where(place == 1, lse - two / one, jnp.where(place == 2, jnp.sqrt(own[:, 0:1]), peak)),
    )
    out[...] = jnp.where(alive, result, 0.0)
    everyone(total, groups, me, lambda *a: post_to(*a).wait_send())


def score(total, groups, rows, count, identity, x, meta, rank, own, weight):
    width = x.shape[1]
    tiles = weight.shape[1] // groups // TILE
    slots = own.shape[0]
    vmem = pl.BlockSpec(memory_space=pltpu.VMEM)
    dma = pltpu.SemaphoreType.DMA
    return pl.pallas_call(
        functools.partial(score_kernel, total, groups, rows, count),
        out_shape=jax.ShapeDtypeStruct((slots, LANES), F32),
        in_specs=[vmem] * 4 + [pl.BlockSpec(memory_space=pl.ANY)],
        out_specs=vmem,
        scratch_shapes=[
            pltpu.VMEM((RING, width, TILE), BF16),
            pltpu.VMEM((2 * tiles, rows, TILE), F32),
            pltpu.VMEM((2 * tiles, rows, TILE), F32),
            pltpu.VMEM((2, rows, TILE), F32),
            pltpu.VMEM((tiles, rows, TILE), jnp.int16),
            pltpu.VMEM((tiles, rows, TILE), jnp.int16),
            pltpu.VMEM((tiles, rows, TILE), F32),
            pltpu.VMEM((rows, LANES), jnp.int32),
        ]
        + [pltpu.VMEM((rows, LANES), F32)] * 6
        + [
            pltpu.VMEM((count, LANES), F32),
            pltpu.VMEM((total, slots, LANES), F32),
            pltpu.VMEM((total, slots, LANES), F32),
            dma((RING,)),
            dma((2 * tiles,)),
            dma((2 * tiles,)),
            dma((tiles,)),
            dma((tiles,)),
            dma((total,)),
            dma((total,)),
        ],
        compiler_params=pltpu.CompilerParams(
            collective_id=identity, has_side_effects=True, vmem_limit_bytes=VMEM_LIMIT
        ),
    )(x, meta, rank, own, weight)


def fast_body(total, groups, hidden, positions, token_ids, lengths, norm_gain, head_weight):
    slots = positions.shape[0]
    count = total * slots
    width = hidden.shape[1] // groups
    caps = [c for c in CAPS if c < count] + [count]
    vmem = pl.BlockSpec(memory_space=pltpu.VMEM)
    dma = pltpu.SemaphoreType.DMA
    message = width // 2 + LANES
    x, meta, rank, own, bucket = pl.pallas_call(
        functools.partial(gather_kernel, total, groups, caps),
        out_shape=(
            jax.ShapeDtypeStruct((count, width), BF16),
            jax.ShapeDtypeStruct((count, LANES), F32),
            jax.ShapeDtypeStruct((count, LANES), F32),
            jax.ShapeDtypeStruct((slots, LANES), F32),
            jax.ShapeDtypeStruct((1,), jnp.int32),
        ),
        in_specs=[vmem] * 5,
        out_specs=(vmem, vmem, vmem, vmem, pl.BlockSpec(memory_space=pltpu.SMEM)),
        scratch_shapes=[
            pltpu.VMEM((groups, 2 * slots, message), BF16),
            pltpu.VMEM((total, 2 * slots, message), BF16),
            dma((total,)),
            dma((total,)),
        ],
        compiler_params=pltpu.CompilerParams(
            collective_id=0, has_side_effects=True, vmem_limit_bytes=32 * 1024 * 1024
        ),
    )(
        hidden,
        positions.reshape(slots, 1),
        token_ids.reshape(slots, 1),
        lengths.reshape(1, 1),
        norm_gain.reshape(1, -1),
    )
    branches = [
        functools.partial(score, total, groups, cap, count, 1 + k) for k, cap in enumerate(caps)
    ]
    result = lax.switch(bucket[0], branches, x, meta, rank, own, head_weight)
    return tuple(result[:, k] for k in range(4))


def joined(part, axis, combine):
    gathered = jax.tree.map(lambda a: lax.all_gather(a, axis), part)

    def take(source):
        return jax.tree.map(lambda a: lax.dynamic_index_in_dim(a, source, 0, False), gathered)

    return lax.fori_loop(
        1, lax.axis_size(axis), lambda source, state: combine(state, take(source)), take(0)
    )


def combine_stats(first, second):
    top = jnp.maximum(first[0], second[0])
    left = jnp.exp(first[0] - top)
    right = jnp.exp(second[0] - top)
    return (
        top,
        first[1] * left + second[1] * right,
        first[2] * left + second[2] * right,
        first[3] + second[3],
    )


def body(hidden, positions, token_ids, lengths, norm_gain, head_weight):
    picked = jnp.take(hidden, positions, axis=0).astype(jnp.float32)
    square_mean = jnp.mean(picked * picked, axis=1)
    normed = (picked * lax.rsqrt(square_mean + 1e-05)[:, None] * norm_gain[None, :]).astype(
        jnp.bfloat16
    )
    whole_rows, whole_ids = (
        lax.all_gather(normed, "vocab", axis=0, tiled=True),
        lax.all_gather(token_ids, "vocab", axis=0, tiled=True),
    )
    weight = lax.all_gather(head_weight, "req", axis=0, tiled=True)
    columns = weight.shape[1]
    first_col = lax.axis_index("vocab") * columns
    count = whole_rows.shape[0]
    blk = min(512, count)
    width = whole_rows.shape[1]
    col_iota = lax.broadcasted_iota(jnp.int32, (blk, columns), 1)

    def block_stats(pair):
        rows, ids = pair
        logits = jnp.dot(rows, weight, preferred_element_type=jnp.float32)
        top = jnp.max(logits, axis=1)
        expo = jnp.exp(logits - top[:, None])
        total = jnp.sum(expo, axis=1)
        weighted = jnp.sum(expo * logits, axis=1)
        local_id = ids - first_col
        chosen = jnp.sum(jnp.where(col_iota == local_id[:, None], logits, 0.0), axis=1)
        return (top, total, weighted, chosen)

    stats = lax.map(
        block_stats,
        (whole_rows.reshape(count // blk, blk, width), whole_ids.reshape(count // blk, blk)),
    )
    top, total, weighted, chosen = [piece.reshape(-1) for piece in stats]
    slots = positions.shape[0]
    merged = joined((top, total, weighted, chosen), "vocab", combine_stats)
    begin = lax.axis_index("vocab") * slots
    top, total, weighted, chosen = [
        lax.dynamic_slice_in_dim(piece, begin, slots) for piece in merged
    ]
    lse = top + jnp.log(total)
    live = (jnp.arange(slots, dtype=jnp.int32) < lengths[0]).astype(jnp.float32)
    logprob = live * (chosen - lse)
    entropy = live * (lse - weighted / total)
    hidden_norm = live * jnp.sqrt(square_mean)
    top_logit = live * top
    return (logprob, entropy, hidden_norm, top_logit)


def solution(mesh):
    groups = mesh.shape["req"]
    total = mesh.shape["vocab"] * groups

    def program(hidden, positions, token_ids, lengths, norm_gain, head_weight):
        fits = (
            groups == 4
            and positions.shape[0] == 8
            and lengths.shape[0] == 1
            and total * positions.shape[0] <= 256
            and head_weight.shape[1] % (groups * TILE) == 0
            and hidden.shape[1] % (groups * 2 * LANES) == 0
        )
        if fits:
            return fast_body(
                total, groups, hidden, positions, token_ids, lengths, norm_gain, head_weight
            )
        return body(hidden, positions, token_ids, lengths, norm_gain, head_weight)

    own = P(("vocab", "req"))
    return jax.shard_map(
        program,
        mesh=mesh,
        in_specs=(P(("vocab", "req"), None), own, own, own, P(), P("req", "vocab")),
        out_specs=(own, own, own, own),
        check_vma=False,
    )
```

```python
import functools

import jax
import jax.numpy as jnp
from jax import lax
from jax.experimental import pallas as pl
from jax.experimental.pallas import tpu as pltpu
from jax.sharding import PartitionSpec as P

MESH = pl.DeviceIdType.MESH
F32 = jnp.float32
BF16 = jnp.bfloat16
LANES = 128
TILE = 256
RING = 6
STEPS = 32000.0
CAPS = (128, 144, 160, 176, 192)
VMEM_LIMIT = 58 * 1024 * 1024


def everyone(total, groups, me, act):
    def step(i, carry):
        target = lax.rem(me + i, total)
        act(i, target, (target // groups, lax.rem(target, groups)))
        return carry

    lax.fori_loop(1, total, step, 0)


def greet(total, groups, me):
    barrier = pltpu.get_barrier_semaphore()
    everyone(
        total,
        groups,
        me,
        lambda i, target, place: pl.semaphore_signal(
            barrier, inc=1, device_id=place, device_id_type=MESH
        ),
    )
    return barrier


def gather_kernel(
    total, groups, caps,
    hidden, positions, ids, lengths, gain,
    rows_out, meta_out, rank_out, own_out, bucket_out,
    message, inbox, send_sem, recv_sem,
):
    v, r = lax.axis_index("vocab"), lax.axis_index("req")
    me = v * groups + r
    barrier = greet(total, groups, me)

    slots = positions.shape[0]
    width = hidden.shape[1]
    part = width // groups
    half = part // 2
    hot = lax.broadcasted_iota(jnp.int32, (slots, hidden.shape[0]), 1) == positions[...]
    picked = jnp.dot(
        hot.astype(F32), hidden[...].astype(F32), preferred_element_type=F32
    )
    square_mean = jnp.sum(picked * picked, axis=1, keepdims=True) * (1.0 / width)
    normed = picked * lax.rsqrt(square_mean + 1e-05) * gain[...]
    normed = normed.astype(BF16).astype(F32)
    grain = []
    for side in range(2):
        bound = jnp.sum(
            jnp.abs(normed[:, side * (width // 2) : (side + 1) * (width // 2)]),
            axis=1, keepdims=True,
        )
        grain.append(bound * (0.5 * (1.0 + 2.0**-7) / STEPS) + 1e-30)
    lane = lax.broadcasted_iota(jnp.int32, (slots, LANES), 1)
    token = ids[...]
    length = lengths[...]
    meta = jnp.zeros((slots, LANES), F32)
    for place, value in enumerate(
        (
            (token & 255).astype(F32),
            ((token >> 8) & 255).astype(F32),
            (token >> 16).astype(F32),
            length.astype(F32),
            grain[0],
            grain[1],
        )
    ):
        meta = jnp.where(lane == place, value, meta)
    meta = jnp.concatenate([meta, jnp.zeros((slots, LANES), F32)], axis=0).astype(BF16)
    for g in range(groups):
        message[g, :, :half] = jnp.concatenate(
            [
                normed[:, g * part : g * part + half],
                normed[:, g * part + half : (g + 1) * part],
            ],
            axis=0,
        ).astype(BF16)
        message[g, :, half:] = meta
    slot = lax.broadcasted_iota(jnp.int32, (slots, LANES), 0)
    alive = (slot < length).astype(F32)
    own_out[...] = jnp.where(lane == 0, square_mean, alive)

    pl.semaphore_wait(barrier, total - 1)

    def copy_to(i, target, place):
        return pltpu.make_async_remote_copy(
            src_ref=message.at[place[1]],
            dst_ref=inbox.at[me],
            send_sem=send_sem.at[i],
            recv_sem=recv_sem.at[me],
            device_id=place,
            device_id_type=MESH,
        )

    def copy_from(i, target, place):
        return pltpu.make_async_remote_copy(
            src_ref=message.at[place[1]],
            dst_ref=inbox.at[target],
            send_sem=send_sem.at[i],
            recv_sem=recv_sem.at[target],
            device_id=place,
            device_id_type=MESH,
        )

    everyone(total, groups, me, lambda *a: copy_to(*a).start())
    inbox[me] = message[r]
    everyone(total, groups, me, lambda *a: copy_from(*a).wait_recv())

    count = total * slots
    got = inbox[...].astype(F32)
    rows = jnp.concatenate(
        [
            got[:, :slots, :half].reshape(count, half),
            got[:, slots:, :half].reshape(count, half),
        ],
        axis=1,
    ).astype(BF16)
    info = got[:, :slots, half:].reshape(count, LANES)
    at = lax.rem(lax.broadcasted_iota(jnp.int32, (count, LANES), 0), slots).astype(F32)
    live = (at < info[:, 3:4]).astype(F32)
    across = lax.broadcasted_iota(jnp.int32, (count, count), 0)
    along = lax.broadcasted_iota(jnp.int32, (count, count), 1)
    live_row = live.T
    rank_row = jnp.dot(
        live_row.astype(BF16), (across < along).astype(F32).astype(BF16),
        preferred_element_type=F32,
    )
    rank_col = jnp.dot(
        (along < across).astype(F32).astype(BF16), live.astype(BF16),
        preferred_element_type=F32,
    )
    rank_out[...] = jnp.where(live > 0.0, rank_col, -1.0)
    goes = jnp.where(live_row[0:1, :] > 0.0, rank_row[0:1, :], -1.0)
    order = (goes == across.astype(F32)).astype(F32).astype(BF16)
    rows_out[...] = jnp.dot(order, rows, preferred_element_type=F32).astype(BF16)
    meta_out[...] = jnp.dot(order, info.astype(BF16), preferred_element_type=F32)
    lives = jnp.sum(live_row[0:1, :]).astype(jnp.int32)
    bucket = jnp.int32(0)
    for cap in caps[:-1]:
        bucket = bucket + (lives > cap).astype(jnp.int32)
    bucket_out[0] = bucket

    everyone(total, groups, me, lambda *a: copy_to(*a).wait_send())


def score_kernel(
    total, groups, rows, count,
    x, meta, rank, own, weight,
    out,
    ring, core_out, core_in, part, side_out, side_in, mine,
    ask, give_scale, take_scale, top, total_sum, weighted, chosen, stats, posts, mail,
    ring_sem, core_send, core_recv, side_send, side_recv, post_send, post_recv,
):
    v, r = lax.axis_index("vocab"), lax.axis_index("req")
    me = v * groups + r
    y, core = r // 2, lax.rem(r, 2)
    twin = y * 2 + (1 - core)
    across = (1 - y) * 2 + core
    diagonal = (1 - y) * 2 + (1 - core)
    columns = weight.shape[1]
    quarter = columns // groups
    tiles = quarter // TILE
    fetches = groups * tiles
    first_half = 2 * tiles

    def fetch(n):
        t = lax.rem(n, first_half) // 2
        odd = lax.rem(n, 2)
        early = (n < first_half).astype(jnp.int32)
        yy = early * (1 - y) + (1 - early) * y
        cc = odd * core + (1 - odd) * (1 - core)
        begin = pl.multiple_of((yy * 2 + cc) * quarter + t * TILE, TILE)
        where = lax.rem(n, RING)
        return pltpu.make_async_copy(
            weight.at[:, pl.ds(begin, TILE)], ring.at[where], ring_sem.at[where]
        )

    for n in range(RING - 1):
        fetch(jnp.int32(n)).start()
    barrier = greet(total, groups, me)

    lane = lax.broadcasted_iota(jnp.int32, (rows, LANES), 1)
    info = meta[:rows, :]
    token = info[:, 0:1] + info[:, 1:2] * 256.0 + info[:, 2:3] * 65536.0
    base = v * columns + r * quarter
    ask[...] = token.astype(jnp.int32) - base - lane
    low = jnp.broadcast_to(info[:, 4:5], (rows, LANES))
    high = jnp.broadcast_to(info[:, 5:6], (rows, LANES))
    is_low = jnp.broadcast_to(y == 0, (rows, LANES))
    give_scale[...] = 1.0 / jnp.where(is_low, low, high)
    take_scale[...] = jnp.where(is_low, high, low)
    top[...] = jnp.full((rows, LANES), -3e38, F32)
    total_sum[...] = jnp.zeros((rows, LANES), F32)
    weighted[...] = jnp.zeros((rows, LANES), F32)
    chosen[...] = jnp.zeros((rows, LANES), F32)
    pl.semaphore_wait(barrier, total - 1)

    def product(n):
        @pl.when(n + (RING - 1) < fetches)
        def _():
            fetch(n + (RING - 1)).start()

        fetch(n).wait()
        return jnp.dot(x[:rows, :], ring[lax.rem(n, RING)], preferred_element_type=F32)

    def core_copy(k):
        return pltpu.make_async_remote_copy(
            src_ref=core_out.at[k],
            dst_ref=core_in.at[k],
            send_sem=core_send.at[k],
            recv_sem=core_recv.at[k],
            device_id=(v, twin),
            device_id_type=MESH,
        )

    def side_copy(t):
        return pltpu.make_async_remote_copy(
            src_ref=side_out.at[t],
            dst_ref=side_in.at[t],
            send_sem=side_send.at[t],
            recv_sem=side_recv.at[t],
            device_id=(v, across),
            device_id_type=MESH,
        )

    blocks = rows // 16

    def hand_over(t):
        core_copy(t).wait_recv()
        held = lax.rem(t, 2)

        def block(b, carry):
            at = pl.ds(pl.multiple_of(b * 16, 16), 16)
            scale = give_scale[at, :]
            for c in range(TILE // LANES):
                cols = pl.ds(c * LANES, LANES)
                value = (part[held, at, cols] + core_in[t, at, cols]) * scale
                side_out[t, at, cols] = jnp.round(value).astype(jnp.int32).astype(jnp.int16)
            return carry

        lax.fori_loop(0, blocks, block, 0)
        side_copy(t).start()

    def early(t, carry):
        core_out[t] = product(2 * t)
        core_copy(t).start()
        part[lax.rem(t, 2)] = product(2 * t + 1)

        @pl.when(t > 0)
        def _():
            hand_over(t - 1)

        return carry

    lax.fori_loop(0, tiles, early, 0)
    hand_over(jnp.int32(tiles - 1))

    def late(t, carry):
        core_out[tiles + t] = product(first_half + 2 * t)
        core_copy(tiles + t).start()
        mine[t] = product(first_half + 2 * t + 1)
        return carry

    lax.fori_loop(0, tiles, late, 0)

    def tally(t, carry):
        core_copy(tiles + t).wait_recv()
        side_copy(t).wait_recv()

        def block(b, inner):
            at = pl.ds(pl.multiple_of(b * 16, 16), 16)
            scale = take_scale[at, :]
            sought = ask[at, :] - t * TILE
            values = []
            for c in range(TILE // LANES):
                cols = pl.ds(c * LANES, LANES)
                far = side_in[t, at, cols].astype(jnp.int32).astype(F32) * scale
                values.append(mine[t, at, cols] + core_in[tiles + t, at, cols] + far)
            before = top[at, :]
            peak = before
            for value in values:
                peak = jnp.maximum(peak, value)
            fade = jnp.exp(before - peak)
            one = total_sum[at, :] * fade
            two = weighted[at, :] * fade
            hit = chosen[at, :]
            for c, value in enumerate(values):
                power = jnp.exp(value - peak)
                one = one + power
                two = two + power * value
                hit = jnp.where(sought == c * LANES, value, hit)
            top[at, :] = peak
            total_sum[at, :] = one
            weighted[at, :] = two
            chosen[at, :] = hit
            return inner

        lax.fori_loop(0, blocks, block, 0)
        return carry

    lax.fori_loop(0, tiles, tally, 0)

    peak = jnp.max(top[...], axis=1, keepdims=True)
    fade = jnp.exp(top[...] - peak)
    one = jnp.sum(total_sum[...] * fade, axis=1, keepdims=True)
    two = jnp.sum(weighted[...] * fade, axis=1, keepdims=True)
    hit = jnp.sum(chosen[...], axis=1, keepdims=True)
    packed = jnp.where(lane == 0, peak, jnp.where(lane == 1, one, jnp.where(lane == 2, two, hit)))
    stats[:rows, :] = packed
    if rows < count:
        stats[rows:, :] = jnp.zeros((count - rows, LANES), F32)
    sought = lax.broadcasted_iota(jnp.int32, (count, count), 1).astype(F32)
    back = (rank[:, 0:1] == sought).astype(F32)
    spread = jnp.dot(
        back, stats[...], preferred_element_type=F32, precision=lax.Precision.HIGHEST
    )
    posts[...] = spread.reshape(posts.shape)

    def post_to(i, target, place):
        return pltpu.make_async_remote_copy(
            src_ref=posts.at[target],
            dst_ref=mail.at[me],
            send_sem=post_send.at[i],
            recv_sem=post_recv.at[me],
            device_id=place,
            device_id_type=MESH,
        )

    def post_from(i, target, place):
        return pltpu.make_async_remote_copy(
            src_ref=posts.at[target],
            dst_ref=mail.at[target],
            send_sem=post_send.at[i],
            recv_sem=post_recv.at[target],
            device_id=place,
            device_id_type=MESH,
        )

    everyone(total, groups, me, lambda *a: post_to(*a).start())
    mail[me] = posts[me]

    def sent(k, carry):
        core_copy(k).wait_send()
        return carry

    lax.fori_loop(0, 2 * tiles, sent, 0)

    def sent_side(t, carry):
        side_copy(t).wait_send()
        return carry

    lax.fori_loop(0, tiles, sent_side, 0)
    everyone(total, groups, me, lambda *a: post_from(*a).wait_recv())

    letters = mail[...]
    tops = letters[:, :, 0:1]
    peak = jnp.max(tops, axis=0)
    fade = jnp.exp(tops - peak[None])
    one = jnp.sum(letters[:, :, 1:2] * fade, axis=0)
    two = jnp.sum(letters[:, :, 2:3] * fade, axis=0)
    hit = jnp.sum(letters[:, :, 3:4], axis=0)
    lse = peak + jnp.log(one)
    alive = own[:, 1:2] > 0.0
    place = lax.broadcasted_iota(jnp.int32, out.shape, 1)
    result = jnp.where(
        place == 0,
        hit - lse,
        jnp.where(place == 1, lse - two / one, jnp.where(place == 2, jnp.sqrt(own[:, 0:1]), peak)),
    )
    out[...] = jnp.where(alive, result, 0.0)
    everyone(total, groups, me, lambda *a: post_to(*a).wait_send())


def score(total, groups, rows, count, identity, x, meta, rank, own, weight):
    width = x.shape[1]
    tiles = weight.shape[1] // groups // TILE
    slots = own.shape[0]
    vmem = pl.BlockSpec(memory_space=pltpu.VMEM)
    dma = pltpu.SemaphoreType.DMA
    return pl.pallas_call(
        functools.partial(score_kernel, total, groups, rows, count),
        out_shape=jax.ShapeDtypeStruct((slots, LANES), F32),
        in_specs=[vmem] * 4 + [pl.BlockSpec(memory_space=pl.ANY)],
        out_specs=vmem,
        scratch_shapes=[
            pltpu.VMEM((RING, width, TILE), BF16),
            pltpu.VMEM((2 * tiles, rows, TILE), F32),
            pltpu.VMEM((2 * tiles, rows, TILE), F32),
            pltpu.VMEM((2, rows, TILE), F32),
            pltpu.VMEM((tiles, rows, TILE), jnp.int16),
            pltpu.VMEM((tiles, rows, TILE), jnp.int16),
            pltpu.VMEM((tiles, rows, TILE), F32),
            pltpu.VMEM((rows, LANES), jnp.int32),
        ]
        + [pltpu.VMEM((rows, LANES), F32)] * 6
        + [
            pltpu.VMEM((count, LANES), F32),
            pltpu.VMEM((total, slots, LANES), F32),
            pltpu.VMEM((total, slots, LANES), F32),
            dma((RING,)),
            dma((2 * tiles,)),
            dma((2 * tiles,)),
            dma((tiles,)),
            dma((tiles,)),
            dma((total,)),
            dma((total,)),
        ],
        compiler_params=pltpu.CompilerParams(
            collective_id=identity, has_side_effects=True, vmem_limit_bytes=VMEM_LIMIT
        ),
    )(x, meta, rank, own, weight)


def fast_body(total, groups, hidden, positions, token_ids, lengths, norm_gain, head_weight):
    slots = positions.shape[0]
    count = total * slots
    width = hidden.shape[1] // groups
    caps = [c for c in CAPS if c < count] + [count]
    vmem = pl.BlockSpec(memory_space=pltpu.VMEM)
    dma = pltpu.SemaphoreType.DMA
    message = width // 2 + LANES
    x, meta, rank, own, bucket = pl.pallas_call(
        functools.partial(gather_kernel, total, groups, caps),
        out_shape=(
            jax.ShapeDtypeStruct((count, width), BF16),
            jax.ShapeDtypeStruct((count, LANES), F32),
            jax.ShapeDtypeStruct((count, LANES), F32),
            jax.ShapeDtypeStruct((slots, LANES), F32),
            jax.ShapeDtypeStruct((1,), jnp.int32),
        ),
        in_specs=[vmem] * 5,
        out_specs=(vmem, vmem, vmem, vmem, pl.BlockSpec(memory_space=pltpu.SMEM)),
        scratch_shapes=[
            pltpu.VMEM((groups, 2 * slots, message), BF16),
            pltpu.VMEM((total, 2 * slots, message), BF16),
            dma((total,)),
            dma((total,)),
        ],
        compiler_params=pltpu.CompilerParams(
            collective_id=0, has_side_effects=True, vmem_limit_bytes=32 * 1024 * 1024
        ),
    )(
        hidden,
        positions.reshape(slots, 1),
        token_ids.reshape(slots, 1),
        lengths.reshape(1, 1),
        norm_gain.reshape(1, -1),
    )
    branches = [
        functools.partial(score, total, groups, cap, count, 1 + k) for k, cap in enumerate(caps)
    ]
    result = lax.switch(bucket[0], branches, x, meta, rank, own, head_weight)
    return tuple(result[:, k] for k in range(4))


def joined(part, axis, combine):
    gathered = jax.tree.map(lambda a: lax.all_gather(a, axis), part)

    def take(source):
        return jax.tree.map(lambda a: lax.dynamic_index_in_dim(a, source, 0, False), gathered)

    return lax.fori_loop(
        1, lax.axis_size(axis), lambda source, state: combine(state, take(source)), take(0)
    )


def combine_stats(first, second):
    top = jnp.maximum(first[0], second[0])
    left = jnp.exp(first[0] - top)
    right = jnp.exp(second[0] - top)
    return (
        top,
        first[1] * left + second[1] * right,
        first[2] * left + second[2] * right,
        first[3] + second[3],
    )


def body(hidden, positions, token_ids, lengths, norm_gain, head_weight):
    picked = jnp.take(hidden, positions, axis=0).astype(jnp.float32)
    square_mean = jnp.mean(picked * picked, axis=1)
    normed = (picked * lax.rsqrt(square_mean + 1e-05)[:, None] * norm_gain[None, :]).astype(
        jnp.bfloat16
    )
    whole_rows, whole_ids = (
        lax.all_gather(normed, "vocab", axis=0, tiled=True),
        lax.all_gather(token_ids, "vocab", axis=0, tiled=True),
    )
    weight = lax.all_gather(head_weight, "req", axis=0, tiled=True)
    columns = weight.shape[1]
    first_col = lax.axis_index("vocab") * columns
    count = whole_rows.shape[0]
    blk = min(512, count)
    width = whole_rows.shape[1]
    col_iota = lax.broadcasted_iota(jnp.int32, (blk, columns), 1)

    def block_stats(pair):
        rows, ids = pair
        logits = jnp.dot(rows, weight, preferred_element_type=jnp.float32)
        top = jnp.max(logits, axis=1)
        expo = jnp.exp(logits - top[:, None])
        total = jnp.sum(expo, axis=1)
        weighted = jnp.sum(expo * logits, axis=1)
        local_id = ids - first_col
        chosen = jnp.sum(jnp.where(col_iota == local_id[:, None], logits, 0.0), axis=1)
        return (top, total, weighted, chosen)

    stats = lax.map(
        block_stats,
        (whole_rows.reshape(count // blk, blk, width), whole_ids.reshape(count // blk, blk)),
    )
    top, total, weighted, chosen = [piece.reshape(-1) for piece in stats]
    slots = positions.shape[0]
    merged = joined((top, total, weighted, chosen), "vocab", combine_stats)
    begin = lax.axis_index("vocab") * slots
    top, total, weighted, chosen = [
        lax.dynamic_slice_in_dim(piece, begin, slots) for piece in merged
    ]
    lse = top + jnp.log(total)
    live = (jnp.arange(slots, dtype=jnp.int32) < lengths[0]).astype(jnp.float32)
    logprob = live * (chosen - lse)
    entropy = live * (lse - weighted / total)
    hidden_norm = live * jnp.sqrt(square_mean)
    top_logit = live * top
    return (logprob, entropy, hidden_norm, top_logit)


def solution(mesh):
    groups = mesh.shape["req"]
    total = mesh.shape["vocab"] * groups

    def program(hidden, positions, token_ids, lengths, norm_gain, head_weight):
        fits = (
            groups == 4
            and positions.shape[0] == 8
            and lengths.shape[0] == 1
            and total * positions.shape[0] <= 256
            and head_weight.shape[1] % (groups * TILE) == 0
            and hidden.shape[1] % (groups * 2 * LANES) == 0
        )
        if fits:
            return fast_body(
                total, groups, hidden, positions, token_ids, lengths, norm_gain, head_weight
            )
        return body(hidden, positions, token_ids, lengths, norm_gain, head_weight)

    own = P(("vocab", "req"))
    return jax.shard_map(
        program,
        mesh=mesh,
        in_specs=(P(("vocab", "req"), None), own, own, own, P(), P("req", "vocab")),
        out_specs=(own, own, own, own),
        check_vma=False,
    )
```
